256 devices in a mesh: ctx: 32 (over z, y), kv: 8 (over x, core).
Axes of the slice: x: 4, y: 4, z: 8, core: 2. Of those that a mesh axis runs over, the one named last changes fastest.
Arguments:
- queries: bfloat16 [8192, 8192], P('ctx', 'kv'), may hold values from -120 to 120
- keys: bfloat16 [8192, 1024], P('ctx', 'kv'), may hold values from -8 to 8
- values: bfloat16 [8192, 1024], P('ctx', 'kv'), may hold values from -6 to 6
- retrieval: int32 [64], P('kv'), may hold values from 0 to 1, as said below
Outputs:
- attention_out: bfloat16 [8192, 8192], P(('ctx', 'kv'))
The draws below stay inside these ranges and needn't reach their ends.
Inputs may be any that keep to these rules, and one draw needn't show every extreme that they name: `retrieval`: exactly 12 of the 64 entries are 1, the rest 0.
All inputs are finite; a program needn't handle non-finite values.
Results may differ from the reference program's by a relative error of at most 0.0045.
Values may be sent and summed in bfloat16 or wider, within the bound.
A program may use at most 64 MiB of HBM per device.

```python
import jax
import jax.numpy as jnp
from jax import lax

HD = 128
HQ = 8
SINK = 64
WINDOW = 4096
RETR = 12
TOKENS = 8192
HEADS = 64
N_KV = 8


def shared_keys(key):
    base = jax.random.normal(key, (TOKENS, N_KV, HD), jnp.float32)
    rows = jnp.arange(TOKENS, dtype=jnp.int32)
    twin = 0.985 * jnp.roll(base, 1, axis=0)
    return jnp.where((rows % 64 == 1)[:, None, None], twin, base)


def draw_keys(key, part):
    common = shared_keys(key)
    return jnp.clip(common, -8.0, 8.0).reshape(TOKENS, N_KV * HD).astype(jnp.bfloat16)


def draw_queries(key, part):
    key = jax.random.fold_in(key, 5)
    first = jax.random.fold_in(key, 0)
    result = jax.random.normal(first, (TOKENS, HEADS, HD), jnp.float32)
    result = jnp.clip(result, -6.0, 6.0)
    result = jnp.clip(result, -120.0, 120.0)
    return result.reshape(TOKENS, HEADS * HD).astype(jnp.bfloat16)


def draw_retrieval(key, part):
    key = jax.random.fold_in(key, 7)
    order = jax.random.permutation(key, HEADS)
    return (order < RETR).astype(jnp.int32)


def levels(stream_key, dims, shards, smallest, largest):
    gain, own = 1.0, jax.random.fold_in(stream_key, 6)
    for position, parts in shards:
        heights = jnp.exp(jax.random.uniform(jax.random.fold_in(own, position), (parts,), jnp.float32, smallest / len(shards), largest / len(shards)))
        gain = gain * jnp.repeat(heights, dims[position] // parts).reshape([-1 if axis == position else 1 for axis in range(len(dims))])
    return gain


def scatter_about(key, dims, spread, most, pieces=(), held_as=jnp.bfloat16):
    drawn = jax.random.normal(key, dims, jnp.float32) * spread
    if len(pieces) > 0:
        drawn = levels(key, dims, pieces, -0.22, 0.18) * drawn
    return jnp.clip(drawn, min=-most, max=most).astype(held_as)


def setup_inputs(seed: int = 0) -> dict:
    key_of = jax.random.split(jax.random.key(seed), 5)
    queries = draw_queries(jax.random.fold_in(key_of[4], 71), 0)
    keys = draw_keys(jax.random.fold_in(key_of[4], 71), 0)
    values = scatter_about(key_of[2], (TOKENS, N_KV * HD), 1.0, 6.0, ((0, 32), (1, 8)))
    retrieval = draw_retrieval(jax.random.fold_in(key_of[4], 71), 0)
    return {"queries": queries, "keys": keys, "values": values, "retrieval": retrieval}


NEG = -1.0e30


def reference(queries, keys, values, retrieval):
    scale = HD ** -0.5
    q_all = queries.reshape(TOKENS, HEADS, HD)
    k_all = keys.reshape(TOKENS, N_KV, HD)
    v_all = values.reshape(TOKENS, N_KV, HD)
    tpos = jnp.arange(TOKENS, dtype=jnp.int32)
    causal = tpos[None, :] <= tpos[:, None]
    near = (tpos[None, :] < SINK) | (tpos[:, None] - tpos[None, :] < WINDOW)

    def one_head(head):
        group = head // HQ
        q_head = q_all[:, head]
        k_head = k_all[:, group]
        v_head = v_all[:, group]
        scores = jnp.dot(q_head, k_head.T, preferred_element_type=jnp.float32) * scale
        allowed = causal & ((retrieval[head] == 1) | near)
        masked = jnp.where(allowed, scores, NEG)
        peak = jnp.max(masked, axis=1)
        weights = jnp.where(allowed, jnp.exp(masked - peak[:, None]), 0.0)
        total = jnp.sum(weights, axis=1)
        numer = jnp.dot(weights.astype(jnp.bfloat16), v_head, preferred_element_type=jnp.float32)
        return (numer / total[:, None]).astype(jnp.bfloat16)

    outs = lax.map(one_head, jnp.arange(HEADS, dtype=jnp.int32))
    return jnp.transpose(outs, (1, 0, 2)).reshape(TOKENS, HEADS * HD)
```

```python
import functools

import jax
import jax.numpy as jnp
from jax import lax
from jax.experimental import pallas as pl
from jax.experimental.pallas import tpu as pltpu
from jax.sharding import PartitionSpec as P

HD = 128
HQ = 8
SINK = 64
WINDOW = 4096
NEG = -1e30
SCALE = HD ** (-0.5) * 1.4426950408889634

NY = 4
NZ = 8
NKV = 8
BLOCK = 256
PLANE = NY * BLOCK
HALF = BLOCK // 2
GROUPS = 4
WIDE = HQ * HD // GROUPS
MESH = pl.DeviceIdType.MESH


def kernel(
    flags, q_ref, k_ref, v_ref, out_ref,
    kbuf, vbuf, peak, total, numer, bias, done,
    y_send, y_recv, z_send, z_recv, x_send, x_recv,
):
    ctx = lax.axis_index("ctx")
    kv = lax.axis_index("kv")
    z = ctx // NY
    y = ctx % NY

    def plane(d):
        return (z + d + NZ) % NZ

    def beside_y(d):
        return (y + d + NY) % NY

    def y_device(d):
        return {"ctx": z * NY + beside_y(d), "kv": kv}

    def z_device(d):
        return {"ctx": plane(d) * NY + y, "kv": kv}

    def x_device(j):
        return {"ctx": ctx, "kv": (kv + j) % NKV}

    barrier = pltpu.get_barrier_semaphore()
    for peer in [y_device(1), y_device(-1), z_device(1), z_device(-1)] + [x_device(j) for j in range(1, NKV)]:
        pl.semaphore_signal(barrier, inc=1, device_id=peer, device_id_type=MESH)

    mine = pl.ds(pl.multiple_of(ctx * BLOCK, BLOCK), BLOCK)
    kbuf[mine, :] = k_ref[...]
    vbuf[mine, :] = v_ref[...]
    pl.semaphore_wait(barrier, 4 + NKV - 1)

    bufs = {"k": kbuf, "v": vbuf}
    started = {}
    y_numbers, z_numbers = {}, {}

    def copy_rows(buf, start, size, peer, sems, number):
        rows = pl.ds(pl.multiple_of(start, HALF), size)
        return pltpu.make_async_remote_copy(
            src_ref=buf.at[rows, :],
            dst_ref=buf.at[rows, :],
            send_sem=sems[0].at[number],
            recv_sem=sems[1].at[number],
            device_id=peer,
            device_id_type=MESH,
        )

    def y_copy(name, d, hop, sign, receive):
        number = y_numbers.setdefault((name, d, hop, sign), len(y_numbers))
        back = hop if receive else hop - 1
        start = (plane(d) * NY + beside_y(-sign * back)) * BLOCK
        size = BLOCK
        if hop == 2:
            size = HALF
            start = start + (0 if sign > 0 else HALF)
        return copy_rows(bufs[name], start, size, y_device(sign), (y_send, y_recv), number)

    def z_copy(name, hop, sign, receive):
        number = z_numbers.setdefault((name, hop, sign), len(z_numbers))
        back = hop if receive else hop - 1
        p = plane(-sign * back)
        if name == "k":
            start, size = (p * NY + y) * BLOCK, BLOCK
        else:
            start, size = p * PLANE, PLANE
        if hop == 4:
            size = size // 2
            start = start + (0 if sign > 0 else size)
        return copy_rows(bufs[name], start, size, z_device(sign), (z_send, z_recv), number)

    def go(maker, *key):
        for sign in (1, -1):
            maker(*key, sign, False).start()
            started[(maker, *key, sign, False)] = None

    def arrive(maker, *key):
        for sign in (1, -1):
            maker(*key, sign, True).wait_recv()

    go(y_copy, "v", 0, 1)
    go(z_copy, "k", 1)
    go(y_copy, "k", 0, 1)

    peak[...] = jnp.full_like(peak, NEG)
    total[...] = jnp.zeros_like(total)
    numer[...] = jnp.zeros_like(numer)

    def compute(p, masked, between=None):
        rows = pl.ds(pl.multiple_of(p * PLANE, PLANE), PLANE)
        scores, weights, fades = {}, {}, {}
        far = p < z - WINDOW // PLANE

        def score(h):
            scores[h] = lax.dot_general(
                q_ref[:, h * HD:(h + 1) * HD], kbuf[rows, :],
                (((1,), (1,)), ((), ())), preferred_element_type=jnp.float32,
            )

        def weigh(h):
            s = scores.pop(h)
            old = peak[h]
            if masked:
                s = s + bias[flags[h]]
                new = jnp.maximum(old, jnp.max(s, axis=1, keepdims=True))
                low = new * SCALE
            else:
                shut = jnp.where(far, (1 - flags[h]).astype(jnp.float32) * NEG, 0.0)
                new = jnp.maximum(old, jnp.max(s, axis=1, keepdims=True) + shut)
                low = new * SCALE - shut
            weights[h] = jnp.exp2(s * SCALE - jnp.tile(low, (1, PLANE // HD))).astype(jnp.bfloat16)
            fades[h] = jnp.exp2((old - new) * SCALE)
            peak[h] = new

        def add(h):
            piece = vbuf[rows, :]
            piece = jnp.concatenate([piece, jnp.ones_like(piece)], axis=1)
            sums = jnp.dot(weights.pop(h), piece, preferred_element_type=jnp.float32)
            fade = fades.pop(h)
            total[h] = total[h] * fade + sums[:, HD:]
            numer[h] = numer[h] * fade + sums[:, :HD]

        score(0)
        for h in range(HQ):
            if h + 1 < HQ:
                score(h + 1)
            weigh(h)
            if h > 0:
                add(h - 1)
            if between is not None and h == HQ // 2 - 1:
                between()
        add(HQ - 1)

    def make_bias(p):
        def some(i, _):
            rows = pl.ds(pl.multiple_of(i * 32, 32), 32)
            t = ctx * BLOCK + i * 32 + lax.broadcasted_iota(jnp.int32, (32, PLANE), 0)
            s = p * PLANE + lax.broadcasted_iota(jnp.int32, (32, PLANE), 1)
            causal = s <= t
            near = (s < SINK) | (t - s < WINDOW)
            bias[1, rows, :] = jnp.where(causal, 0.0, NEG)
            bias[0, rows, :] = jnp.where(causal & near, 0.0, NEG)
            return 0

        lax.fori_loop(0, BLOCK // 32, some, 0)

    arrive(y_copy, "v", 0, 1)
    go(y_copy, "v", 0, 2)
    arrive(z_copy, "k", 1)
    go(z_copy, "k", 2)
    arrive(y_copy, "k", 0, 1)
    go(y_copy, "k", 0, 2)
    go(y_copy, "k", 1, 1)
    go(y_copy, "k", -1, 1)
    arrive(y_copy, "v", 0, 2)
    go(z_copy, "v", 1)
    arrive(y_copy, "k", 0, 2)

    def step(i):
        if i == 1:
            arrive(y_copy, "k", 1, 1)
            go(y_copy, "k", 1, 2)
            arrive(y_copy, "k", -1, 1)
            go(y_copy, "k", -1, 2)
            arrive(z_copy, "k", 2)
            go(z_copy, "k", 3)
            go(y_copy, "k", 2, 1)
            go(y_copy, "k", -2, 1)
            arrive(z_copy, "v", 1)
            go(z_copy, "v", 2)
            arrive(y_copy, "k", 1, 2)
            arrive(y_copy, "k", -1, 2)
        elif i == 2:
            arrive(y_copy, "k", 2, 1)
            go(y_copy, "k", 2, 2)
            arrive(y_copy, "k", -2, 1)
            go(y_copy, "k", -2, 2)
            arrive(z_copy, "k", 3)
            go(z_copy, "k", 4)
            go(y_copy, "k", 3, 1)
            go(y_copy, "k", -3, 1)
        elif i == 3:
            arrive(z_copy, "v", 2)
            go(z_copy, "v", 3)
            arrive(y_copy, "k", 2, 2)
            arrive(y_copy, "k", -2, 2)
        elif i == 4:
            arrive(y_copy, "k", 3, 1)
            go(y_copy, "k", 3, 2)
            arrive(y_copy, "k", -3, 1)
            go(y_copy, "k", -3, 2)
            arrive(z_copy, "k", 4)
            go(y_copy, "k", 4, 1)
        elif i == 5:
            arrive(z_copy, "v", 3)
            go(z_copy, "v", 4)
            arrive(y_copy, "k", 3, 2)
            arrive(y_copy, "k", -3, 2)
        elif i == 6:
            arrive(y_copy, "k", 4, 1)
            go(y_copy, "k", 4, 2)
        elif i == 7:
            arrive(z_copy, "v", 4)
            arrive(y_copy, "k", 4, 2)

    def one(i, _):
        for k in range(1, NZ):
            pl.when(i == k)(functools.partial(step, k))
        ring = (i + 1) // 2
        p = (z + jnp.where(i % 2 == 0, ring, -ring) + NZ) % NZ
        edge = z - WINDOW // PLANE
        masked = (p == z) | (p == edge) | ((p == 0) & (edge > 0))

        @pl.when((p <= z) & masked)
        def _():
            make_bias(p)
            compute(p, True)

        @pl.when((p <= z) & jnp.logical_not(masked))
        def _():
            compute(p, False)

        return 0

    lax.fori_loop(0, NZ, one, 0)

    def x_copy(j, g, receive):
        number = (j - 1) * GROUPS + g
        rows = (kv + j) % NKV * (BLOCK // NKV)
        columns = ((kv - j + NKV) % NKV if receive else kv) * (HQ * HD) + g * WIDE
        return pltpu.make_async_remote_copy(
            src_ref=done.at[pl.ds(pl.multiple_of(rows, BLOCK // NKV), BLOCK // NKV), pl.ds(g * WIDE, WIDE)],
            dst_ref=out_ref.at[:, pl.ds(pl.multiple_of(columns, WIDE), WIDE)],
            send_sem=x_send.at[number],
            recv_sem=x_recv.at[number],
            device_id=x_device(j),
            device_id_type=MESH,
        )

    for g in range(GROUPS):
        for h in range(g * HQ // GROUPS, (g + 1) * HQ // GROUPS):
            done[:, h * HD:(h + 1) * HD] = (numer[h] / total[h]).astype(jnp.bfloat16)
        for j in range(1, NKV):
            x_copy(j, g, False).start()
            started[(x_copy, j, g, False)] = None
    own = pl.ds(pl.multiple_of(kv * (BLOCK // NKV), BLOCK // NKV), BLOCK // NKV)
    out_ref[:, pl.ds(pl.multiple_of(kv * (HQ * HD), HQ * HD), HQ * HD)] = done[own, :]
    for g in range(GROUPS):
        for j in range(1, NKV):
            x_copy(j, g, True).wait_recv()
    for maker, *key in started:
        maker(*key).wait_send()


def shards(queries, keys, values, retrieval):
    rows = queries.shape[0]
    vmem = pl.BlockSpec(memory_space=pltpu.VMEM)
    state = pltpu.VMEM((HQ, rows, HD), jnp.float32)
    n_y = 2 * 2 * (1 + NZ)
    n_z = 2 * 2 * 4
    n_x = (NKV - 1) * GROUPS
    return pl.pallas_call(
        kernel,
        out_shape=jax.ShapeDtypeStruct((rows // NKV, NKV * HQ * HD), jnp.bfloat16),
        in_specs=[pl.BlockSpec(memory_space=pltpu.SMEM), vmem, vmem, vmem],
        out_specs=vmem,
        scratch_shapes=[
            pltpu.VMEM((NZ * PLANE, HD), jnp.bfloat16),
            pltpu.VMEM((NZ * PLANE, HD), jnp.bfloat16),
            state, state, state,
            pltpu.VMEM((2, rows, PLANE), jnp.float32),
            pltpu.VMEM((rows, HQ * HD), jnp.bfloat16),
            pltpu.SemaphoreType.DMA((n_y,)),
            pltpu.SemaphoreType.DMA((n_y,)),
            pltpu.SemaphoreType.DMA((n_z,)),
            pltpu.SemaphoreType.DMA((n_z,)),
            pltpu.SemaphoreType.DMA((n_x,)),
            pltpu.SemaphoreType.DMA((n_x,)),
        ],
        compiler_params=pltpu.CompilerParams(
            collective_id=0, has_side_effects=True, vmem_limit_bytes=48 * 1024 * 1024
        ),
    )(retrieval, queries, keys, values)


def solution(mesh):
    return jax.shard_map(
        shards,
        mesh=mesh,
        in_specs=(P("ctx", "kv"), P("ctx", "kv"), P("ctx", "kv"), P("kv")),
        out_specs=P(("ctx", "kv"), None),
        check_vma=False,
    )
```

```python
import functools

import jax
import jax.numpy as jnp
from jax import lax
from jax.experimental import pallas as pl
from jax.experimental.pallas import tpu as pltpu
from jax.sharding import PartitionSpec as P

HD = 128
HQ = 8
SINK = 64
WINDOW = 4096
NEG = -1e30
SCALE = HD ** (-0.5) * 1.4426950408889634

NY = 4
NZ = 8
NKV = 8
PARTS = {"k": 2, "v": NY}
BLOCK = 256
PLANE = NY * BLOCK
HALF = BLOCK // 2
GROUPS = 4
WIDE = HQ * HD // GROUPS
MESH = pl.DeviceIdType.MESH


def kernel(
    flags_hbm, q_hbm, k_hbm, v_hbm, out_ref,
    flags, q_ref, kbuf, vbuf, peak, total, numer, bias, done,
    local_sem, y_send, y_recv, z_send, z_recv, x_send, x_recv,
):
    ctx = lax.axis_index("ctx")
    kv = lax.axis_index("kv")
    z = ctx // NY
    y = ctx % NY

    def plane(d):
        return (z + d + NZ) % NZ

    def beside(d):
        return (y + d + NY) % NY

    def y_device(d):
        return {"ctx": z * NY + beside(d), "kv": kv}

    def z_device(d):
        return {"ctx": plane(d) * NY + y, "kv": kv}

    def x_device(j):
        return {"ctx": ctx, "kv": (kv + j) % NKV}

    barrier = pltpu.get_barrier_semaphore()

    def greet(peer):
        pl.semaphore_signal(barrier, inc=1, device_id=peer, device_id_type=MESH)

    for d in range(1, NY):
        greet(y_device(d))
    for j in range(1, NKV):
        greet(x_device(j))
    pl.when(z > 0)(functools.partial(greet, z_device(-1)))
    pl.when((z != NZ // 2 - 1))(functools.partial(greet, z_device(1)))
    expected = NY - 1 + NKV - 1 + jnp.where(z < NZ - 1, 1, 0) + jnp.where(z != NZ // 2, 1, 0)

    def rows_of(start, size):
        return pl.ds(pl.multiple_of(start, HALF), size)

    mine = rows_of(ctx * BLOCK, BLOCK)
    local = [
        pltpu.make_async_copy(v_hbm, vbuf.at[mine, :], local_sem.at[0]),
        pltpu.make_async_copy(k_hbm, kbuf.at[mine, :], local_sem.at[1]),
        pltpu.make_async_copy(flags_hbm, flags, local_sem.at[2]),
        pltpu.make_async_copy(q_hbm, q_ref, local_sem.at[3]),
    ]
    for copy in local:
        copy.start()
    pl.semaphore_wait(barrier, expected)

    bufs = {"k": kbuf, "v": vbuf}
    started = {}
    numbers = {}

    def remote(src, dst, peer, sems, key):
        count = len([k for k in numbers if k[0] == key[0]])
        number = numbers.setdefault(key, count)
        return pltpu.make_async_remote_copy(
            src_ref=src,
            dst_ref=dst,
            send_sem=sems[0].at[number],
            recv_sem=sems[1].at[number],
            device_id=peer,
            device_id_type=MESH,
        )

    def y_copy(name, d, way, receive):
        rows = rows_of((plane(d) * NY + (beside(-way) if receive else y)) * BLOCK, BLOCK)
        dst = bufs[name].at[rows, :]
        src = {"k": k_hbm, "v": v_hbm}[name] if d == 0 else dst
        return remote(src, dst, y_device(way), (y_send, y_recv), ("y", name, d, way))

    def z_copy(name, hop, sign, part, receive):
        p = plane(-sign * (hop if receive else hop - 1))
        if name == "k":
            rows = rows_of((p * NY + y) * BLOCK + part * HALF, HALF)
        else:
            rows = rows_of((p * NY + beside(part)) * BLOCK, BLOCK)
        ref = bufs[name].at[rows, :]
        src = ref
        if hop == 1 and not receive:
            if name == "k":
                src = k_hbm.at[pl.ds(part * HALF, HALF), :]
            elif part == 0:
                src = v_hbm
        return remote(src, ref, z_device(sign), (z_send, z_recv), ("z", name, hop, sign, part))

    def last_hop(name, sign, part):
        return NZ // 2 if (part < PARTS[name] // 2) == (sign > 0) else NZ // 2 - 1

    def needed(name, hop, sign, part, receive):
        if sign > 0:
            return z >= hop if receive else (z >= hop - 1) & (z < NZ - 1)
        return plane(hop if receive else hop - 1) < last_hop(name, sign, part)

    def go(maker, *key, when=None):
        def start():
            maker(*key, False).start()

        def end():
            maker(*key, False).wait_send()

        if when is None:
            start()
        else:
            pl.when(when())(start)
        started[(maker, *key)] = (end, when)

    def arrive(maker, *key, when=None):
        def wait():
            maker(*key, True).wait_recv()

        if when is None:
            wait()
        else:
            pl.when(when())(wait)

    def go_y(name, back):
        for way in (1, -1, 2):
            go(y_copy, name, -back, way, when=lambda: z >= back)

    def arrive_y(name, back):
        for way in (1, -1, 2):
            arrive(y_copy, name, -back, way, when=lambda: z >= back)

    def send_on(name, hop, sign, part):
        if hop <= last_hop(name, sign, part):
            go(z_copy, name, hop, sign, part, when=functools.partial(needed, name, hop, sign, part, False))

    def pass_on(name, hop):
        for part in range(PARTS[name]):
            for sign in (1, -1):
                if hop <= last_hop(name, sign, part):
                    arrive(z_copy, name, hop, sign, part, when=functools.partial(needed, name, hop, sign, part, True))
                    send_on(name, hop + 1, sign, part)

    go_y("v", 0)
    for sign in (1, -1):
        for part in range(PARTS["k"]):
            send_on("k", 1, sign, part)
        send_on("v", 1, sign, 0)
    go_y("k", 0)

    peak[...] = jnp.full_like(peak, NEG)
    total[...] = jnp.zeros_like(total)
    numer[...] = jnp.zeros_like(numer)

    def compute(p, masked, after=None):
        rows = pl.ds(pl.multiple_of(p * PLANE, PLANE), PLANE)
        scores, weights, fades = {}, {}, {}
        far = p < z - WINDOW // PLANE

        def score(h):
            scores[h] = lax.dot_general(
                q_ref[:, h * HD:(h + 1) * HD], kbuf[rows, :],
                (((1,), (1,)), ((), ())), preferred_element_type=jnp.float32,
            )

        def weigh(h):
            s = scores.pop(h)
            old = peak[h]
            if masked:
                s = s + bias[flags[h]]
                new = jnp.maximum(old, jnp.max(s, axis=1, keepdims=True))
                low = new * SCALE
            else:
                shut = jnp.where(far, (1 - flags[h]).astype(jnp.float32) * NEG, 0.0)
                new = jnp.maximum(old, jnp.max(s, axis=1, keepdims=True) + shut)
                low = new * SCALE - shut
            weights[h] = jnp.exp2(s * SCALE - jnp.tile(low, (1, PLANE // HD))).astype(jnp.bfloat16)
            fades[h] = jnp.exp2((old - new) * SCALE)
            peak[h] = new

        def add(h):
            piece = vbuf[rows, :]
            piece = jnp.concatenate([piece, jnp.ones_like(piece)], axis=1)
            sums = jnp.dot(weights.pop(h), piece, preferred_element_type=jnp.float32)
            fade = fades.pop(h)
            total[h] = total[h] * fade + sums[:, HD:]
            numer[h] = numer[h] * fade + sums[:, :HD]

        score(0)
        for h in range(HQ):
            if h + 1 < HQ:
                score(h + 1)
            weigh(h)
            if h > 0:
                add(h - 1)
                if after is not None:
                    after(h - 1)
        add(HQ - 1)
        if after is not None:
            after(HQ - 1)

    def make_bias(p):
        def some(i, _):
            rows = pl.ds(pl.multiple_of(i * 32, 32), 32)
            t = ctx * BLOCK + i * 32 + lax.broadcasted_iota(jnp.int32, (32, PLANE), 0)
            s = p * PLANE + lax.broadcasted_iota(jnp.int32, (32, PLANE), 1)
            causal = s <= t
            near = (s < SINK) | (t - s < WINDOW)
            bias[1, rows, :] = jnp.where(causal, 0.0, NEG)
            bias[0, rows, :] = jnp.where(causal & near, 0.0, NEG)
            return 0

        lax.fori_loop(0, BLOCK // 32, some, 0)

    make_bias(z)
    for copy in local:
        copy.wait()
    pass_on("k", 1)
    go_y("k", 1)
    arrive_y("v", 0)
    for part in range(1, PARTS["v"]):
        for sign in (1, -1):
            send_on("v", 1, sign, part)
    arrive_y("k", 0)
    go_y("k", 7)
    compute(z, True)

    def step(i):
        if i == 1:
            pass_on("k", 2)
            go_y("k", 2)
            go_y("k", 6)
            pass_on("v", 1)
            arrive_y("k", 1)
        elif i == 2:
            pass_on("k", 3)
            go_y("k", 3)
            go_y("k", 5)
            arrive_y("k", 7)
        elif i == 3:
            pass_on("v", 2)
            pass_on("k", 4)
            go_y("k", 4)
            arrive_y("k", 2)
        elif i == 4:
            arrive_y("k", 6)
        elif i == 5:
            pass_on("v", 3)
            arrive_y("k", 3)
        elif i == 6:
            arrive_y("k", 5)

    edge = z - WINDOW // PLANE

    def one(i, _):
        for k in range(1, NZ - 1):
            pl.when(i == k)(functools.partial(step, k))
        ring = (i + 1) // 2
        p = (z + jnp.where(i % 2 == 0, ring, -ring) + NZ) % NZ
        masked = (p == 0) & (edge > 0)

        @pl.when((p < z) & masked)
        def _():
            make_bias(p)
            compute(p, True)

        @pl.when((p < z) & jnp.logical_not(masked))
        def _():
            compute(p, False)

        return 0

    lax.fori_loop(1, NZ - 1, one, 0)

    def x_copy(j, g, receive):
        rows = (kv + j) % NKV * (BLOCK // NKV)
        columns = ((kv - j + NKV) % NKV if receive else kv) * (HQ * HD) + g * WIDE
        return remote(
            done.at[pl.ds(pl.multiple_of(rows, BLOCK // NKV), BLOCK // NKV), pl.ds(g * WIDE, WIDE)],
            out_ref.at[:, pl.ds(pl.multiple_of(columns, WIDE), WIDE)],
            x_device(j), (x_send, x_recv), ("x", j, g),
        )

    def finish(h):
        done[:, h * HD:(h + 1) * HD] = (numer[h] / total[h]).astype(jnp.bfloat16)
        if (h + 1) % (HQ // GROUPS) == 0:
            for j in range(1, NKV):
                go(x_copy, j, h // (HQ // GROUPS))

    pass_on("v", NZ // 2)
    arrive_y("k", 4)

    @pl.when(edge >= 0)
    def _():
        make_bias(edge)
        compute(edge, True, finish)

    @pl.when(edge < 0)
    def _():
        for h in range(HQ):
            finish(h)

    own = pl.ds(pl.multiple_of(kv * (BLOCK // NKV), BLOCK // NKV), BLOCK // NKV)
    out_ref[:, pl.ds(pl.multiple_of(kv * (HQ * HD), HQ * HD), HQ * HD)] = done[own, :]
    for g in range(GROUPS):
        for j in range(1, NKV):
            arrive(x_copy, j, g)
    for end, when in started.values():
        if when is None:
            end()
        else:
            pl.when(when())(end)


def shards(queries, keys, values, retrieval):
    rows = queries.shape[0]
    state = pltpu.VMEM((HQ, rows, HD), jnp.float32)
    n_y = (NY - 1) * (1 + NZ)
    n_z = (PARTS["k"] + PARTS["v"]) * 7
    n_x = (NKV - 1) * GROUPS
    return pl.pallas_call(
        kernel,
        out_shape=jax.ShapeDtypeStruct((rows // NKV, NKV * HQ * HD), jnp.bfloat16),
        in_specs=[pl.BlockSpec(memory_space=pltpu.HBM)] * 4,
        out_specs=pl.BlockSpec(memory_space=pltpu.VMEM),
        scratch_shapes=[
            pltpu.SMEM((HQ,), jnp.int32),
            pltpu.VMEM((rows, HQ * HD), jnp.bfloat16),
            pltpu.VMEM((NZ * PLANE, HD), jnp.bfloat16),
            pltpu.VMEM((NZ * PLANE, HD), jnp.bfloat16),
            state, state, state,
            pltpu.VMEM((2, rows, PLANE), jnp.float32),
            pltpu.VMEM((rows, HQ * HD), jnp.bfloat16),
            pltpu.SemaphoreType.DMA((4,)),
            pltpu.SemaphoreType.DMA((n_y,)),
            pltpu.SemaphoreType.DMA((n_y,)),
            pltpu.SemaphoreType.DMA((n_z,)),
            pltpu.SemaphoreType.DMA((n_z,)),
            pltpu.SemaphoreType.DMA((n_x,)),
            pltpu.SemaphoreType.DMA((n_x,)),
        ],
        compiler_params=pltpu.CompilerParams(
            collective_id=0, has_side_effects=True, vmem_limit_bytes=62 * 1024 * 1024
        ),
    )(retrieval, queries, keys, values)


def solution(mesh):
    return jax.shard_map(
        shards,
        mesh=mesh,
        in_specs=(P("ctx", "kv"), P("ctx", "kv"), P("ctx", "kv"), P("kv")),
        out_specs=P(("ctx", "kv"), None),
        check_vma=False,
    )
```

```python
import functools

import jax
import jax.numpy as jnp
from jax import lax
from jax.experimental import pallas as pl
from jax.experimental.pallas import tpu as pltpu
from jax.sharding import PartitionSpec as P

HD = 128
HQ = 8
SINK = 64
WINDOW = 4096
NEG = -1e30
SCALE = HD ** (-0.5) * 1.4426950408889634

NY = 4
NZ = 8
NKV = 8
PARTS = {"k": 2, "v": NY}
BLOCK = 256
PLANE = NY * BLOCK
HALF = BLOCK // 2
GROUPS = 4
WIDE = HQ * HD // GROUPS
MESH = pl.DeviceIdType.MESH


def kernel(
    flags_hbm, q_hbm, k_hbm, v_hbm, out_ref,
    flags, q_ref, kbuf, vbuf, peak, total, numer, own_bias, edge_bias, done,
    local_sem, y_send, y_recv, z_send, z_recv, x_send, x_recv,
):
    ctx = lax.axis_index("ctx")
    kv = lax.axis_index("kv")
    z = ctx // NY
    y = ctx % NY

    def plane(d):
        return (z + d + NZ) % NZ

    def beside(d):
        return (y + d + NY) % NY

    def y_device(d):
        return {"ctx": z * NY + beside(d), "kv": kv}

    def z_device(d):
        return {"ctx": plane(d) * NY + y, "kv": kv}

    def x_device(j):
        return {"ctx": ctx, "kv": (kv + j) % NKV}

    barrier = pltpu.get_barrier_semaphore()

    def greet(peer):
        pl.semaphore_signal(barrier, inc=1, device_id=peer, device_id_type=MESH)

    for d in range(1, NY):
        greet(y_device(d))
    for j in range(1, NKV):
        greet(x_device(j))
    pl.when(z > 0)(functools.partial(greet, z_device(-1)))
    pl.when((z != NZ // 2 - 1))(functools.partial(greet, z_device(1)))
    expected = NY - 1 + NKV - 1 + jnp.where(z < NZ - 1, 1, 0) + jnp.where(z != NZ // 2, 1, 0)

    def rows_of(start, size):
        return pl.ds(pl.multiple_of(start, HALF), size)

    mine = rows_of(ctx * BLOCK, BLOCK)
    local = [
        pltpu.make_async_copy(v_hbm, vbuf.at[mine, :], local_sem.at[0]),
        pltpu.make_async_copy(k_hbm, kbuf.at[mine, :], local_sem.at[1]),
        pltpu.make_async_copy(flags_hbm, flags, local_sem.at[2]),
        pltpu.make_async_copy(q_hbm, q_ref, local_sem.at[3]),
    ]
    for copy in local:
        copy.start()
    pl.semaphore_wait(barrier, expected)

    bufs = {"k": kbuf, "v": vbuf}
    started = {}
    numbers = {}

    def remote(src, dst, peer, sems, key):
        count = len([k for k in numbers if k[0] == key[0]])
        number = numbers.setdefault(key, count)
        return pltpu.make_async_remote_copy(
            src_ref=src,
            dst_ref=dst,
            send_sem=sems[0].at[number],
            recv_sem=sems[1].at[number],
            device_id=peer,
            device_id_type=MESH,
        )

    def y_copy(name, d, way, receive):
        rows = rows_of((plane(d) * NY + (beside(-way) if receive else y)) * BLOCK, BLOCK)
        dst = bufs[name].at[rows, :]
        src = {"k": k_hbm, "v": v_hbm}[name] if d == 0 else dst
        return remote(src, dst, y_device(way), (y_send, y_recv), ("y", name, d, way))

    def z_copy(name, hop, sign, part, receive):
        p = plane(-sign * (hop if receive else hop - 1))
        if name == "k":
            rows = rows_of((p * NY + y) * BLOCK + part * HALF, HALF)
        else:
            rows = rows_of((p * NY + beside(part)) * BLOCK, BLOCK)
        ref = bufs[name].at[rows, :]
        src = ref
        if hop == 1 and not receive:
            if name == "k":
                src = k_hbm.at[pl.ds(part * HALF, HALF), :]
            elif part == 0:
                src = v_hbm
        return remote(src, ref, z_device(sign), (z_send, z_recv), ("z", name, hop, sign, part))

    def last_hop(name, sign, part):
        return NZ // 2 if (part < PARTS[name] // 2) == (sign > 0) else NZ // 2 - 1

    def needed(name, hop, sign, part, receive):
        if sign > 0:
            return z >= hop if receive else (z >= hop - 1) & (z < NZ - 1)
        return plane(hop if receive else hop - 1) < last_hop(name, sign, part)

    def go(maker, *key, when=None):
        def start():
            maker(*key, False).start()

        def end():
            maker(*key, False).wait_send()

        if when is None:
            start()
        else:
            pl.when(when())(start)
        started[(maker, *key)] = (end, when)

    def arrive(maker, *key, when=None):
        def wait():
            maker(*key, True).wait_recv()

        if when is None:
            wait()
        else:
            pl.when(when())(wait)

    def go_y(name, back):
        for way in (1, -1, 2):
            go(y_copy, name, -back, way, when=lambda: z >= back)

    def arrive_y(name, back):
        for way in (1, -1, 2):
            arrive(y_copy, name, -back, way, when=lambda: z >= back)

    def send_on(name, hop, sign, part):
        if hop <= last_hop(name, sign, part):
            go(z_copy, name, hop, sign, part, when=functools.partial(needed, name, hop, sign, part, False))

    def pass_on(name, hop):
        for part in range(PARTS[name]):
            for sign in (1, -1):
                if hop <= last_hop(name, sign, part):
                    arrive(z_copy, name, hop, sign, part, when=functools.partial(needed, name, hop, sign, part, True))
                    send_on(name, hop + 1, sign, part)

    go_y("v", 0)
    for sign in (1, -1):
        for part in range(PARTS["k"]):
            send_on("k", 1, sign, part)
        send_on("v", 1, sign, 0)
    go_y("k", 0)

    peak[...] = jnp.full_like(peak, NEG)
    total[...] = jnp.zeros_like(total)
    numer[...] = jnp.zeros_like(numer)

    def compute(start, size, term, after=None):
        rows = pl.ds(pl.multiple_of(start, BLOCK), size)
        scores, weights, fades = {}, {}, {}

        def score(h):
            scores[h] = lax.dot_general(
                q_ref[:, h * HD:(h + 1) * HD], kbuf[rows, :],
                (((1,), (1,)), ((), ())), preferred_element_type=jnp.float32,
            )

        def weigh(h):
            s = scores.pop(h) + term(h)
            old = peak[h]
            new = jnp.maximum(old, jnp.max(s, axis=1, keepdims=True))
            weights[h] = jnp.exp2(s * SCALE - jnp.tile(new * SCALE, (1, size // HD))).astype(jnp.bfloat16)
            fades[h] = jnp.exp2((old - new) * SCALE)
            peak[h] = new

        def add(h):
            piece = vbuf[rows, :]
            piece = jnp.concatenate([piece, jnp.ones_like(piece)], axis=1)
            sums = jnp.dot(weights.pop(h), piece, preferred_element_type=jnp.float32)
            fade = fades.pop(h)
            total[h] = total[h] * fade + sums[:, HD:]
            numer[h] = numer[h] * fade + sums[:, :HD]

        score(0)
        for h in range(HQ):
            if h + 1 < HQ:
                score(h + 1)
            weigh(h)
            if h > 0:
                add(h - 1)
                if after is not None:
                    after(h - 1)
        add(HQ - 1)
        if after is not None:
            after(HQ - 1)

    edge = z - WINDOW // PLANE

    def shut(h):
        return (1 - flags[h]).astype(jnp.float32) * NEG

    def block_of_own():
        compute(ctx * BLOCK, BLOCK, lambda h: own_bias[...])

    def blocks_before():
        column = lax.broadcasted_iota(jnp.int32, (1, PLANE - BLOCK), 1)
        row = jnp.where(column < y * BLOCK, 0.0, NEG)
        compute(z * PLANE, PLANE - BLOCK, lambda h: row)

    def whole_plane(p):
        column = lax.broadcasted_iota(jnp.int32, (1, PLANE), 1)
        row = jnp.where((p < edge) & (p * PLANE + column >= SINK), 1.0, 0.0)
        compute(p * PLANE, PLANE, lambda h: row * shut(h))

    def edge_plane(after):
        compute(edge * PLANE, PLANE, lambda h: edge_bias[flags[h]], after)

    own_bias[...] = jnp.where(
        lax.broadcasted_iota(jnp.int32, (BLOCK, BLOCK), 1) <= lax.broadcasted_iota(jnp.int32, (BLOCK, BLOCK), 0), 0.0, NEG
    )
    for copy in local:
        copy.wait()
    block_of_own()

    def some(i, _):
        rows = pl.ds(pl.multiple_of(i * 32, 32), 32)
        t = y * BLOCK + i * 32 + lax.broadcasted_iota(jnp.int32, (32, PLANE), 0)
        s = lax.broadcasted_iota(jnp.int32, (32, PLANE), 1)
        edge_bias[0, rows, :] = jnp.where((s > t) | (edge * PLANE + s < SINK), 0.0, NEG)
        edge_bias[1, rows, :] = jnp.zeros((32, PLANE), jnp.float32)
        return 0

    lax.fori_loop(0, BLOCK // 32, some, 0)
    pass_on("k", 1)
    go_y("k", 1)
    arrive_y("v", 0)
    for part in range(1, PARTS["v"]):
        for sign in (1, -1):
            send_on("v", 1, sign, part)
    arrive_y("k", 0)
    go_y("k", 7)
    pl.when(y > 0)(blocks_before)

    def step(i):
        if i == 1:
            pass_on("k", 2)
            go_y("k", 2)
            go_y("k", 6)
            pass_on("v", 1)
            arrive_y("k", 1)
        elif i == 2:
            pass_on("k", 3)
            go_y("k", 3)
            go_y("k", 5)
            arrive_y("k", 7)
        elif i == 3:
            pass_on("v", 2)
            pass_on("k", 4)
            go_y("k", 4)
            arrive_y("k", 2)
        elif i == 4:
            arrive_y("k", 6)
        elif i == 5:
            pass_on("v", 3)
            arrive_y("k", 3)
        elif i == 6:
            arrive_y("k", 5)

    def one(i, _):
        for k in range(1, NZ - 1):
            pl.when(i == k)(functools.partial(step, k))
        ring = (i + 1) // 2
        p = (z + jnp.where(i % 2 == 0, ring, -ring) + NZ) % NZ
        pl.when(p < z)(functools.partial(whole_plane, p))
        return 0

    lax.fori_loop(1, NZ - 1, one, 0)

    def x_copy(j, g, receive):
        rows = (kv + j) % NKV * (BLOCK // NKV)
        columns = ((kv - j + NKV) % NKV if receive else kv) * (HQ * HD) + g * WIDE
        return remote(
            done.at[pl.ds(pl.multiple_of(rows, BLOCK // NKV), BLOCK // NKV), pl.ds(g * WIDE, WIDE)],
            out_ref.at[:, pl.ds(pl.multiple_of(columns, WIDE), WIDE)],
            x_device(j), (x_send, x_recv), ("x", j, g),
        )

    def finish(h):
        done[:, h * HD:(h + 1) * HD] = (numer[h] / total[h]).astype(jnp.bfloat16)
        if (h + 1) % (HQ // GROUPS) == 0:
            for j in range(1, NKV):
                go(x_copy, j, h // (HQ // GROUPS))

    pass_on("v", NZ // 2)
    arrive_y("k", 4)

    @pl.when(edge >= 0)
    def _():
        edge_plane(finish)

    @pl.when(edge < 0)
    def _():
        for h in range(HQ):
            finish(h)

    own = pl.ds(pl.multiple_of(kv * (BLOCK // NKV), BLOCK // NKV), BLOCK // NKV)
    out_ref[:, pl.ds(pl.multiple_of(kv * (HQ * HD), HQ * HD), HQ * HD)] = done[own, :]
    for g in range(GROUPS):
        for j in range(1, NKV):
            arrive(x_copy, j, g)
    for end, when in started.values():
        if when is None:
            end()
        else:
            pl.when(when())(end)


def shards(queries, keys, values, retrieval):
    rows = queries.shape[0]
    state = pltpu.VMEM((HQ, rows, HD), jnp.float32)
    n_y = (NY - 1) * (1 + NZ)
    n_z = (PARTS["k"] + PARTS["v"]) * 7
    n_x = (NKV - 1) * GROUPS
    return pl.pallas_call(
        kernel,
        out_shape=jax.ShapeDtypeStruct((rows // NKV, NKV * HQ * HD), jnp.bfloat16),
        in_specs=[pl.BlockSpec(memory_space=pltpu.HBM)] * 4,
        out_specs=pl.BlockSpec(memory_space=pltpu.VMEM),
        scratch_shapes=[
            pltpu.SMEM((HQ,), jnp.int32),
            pltpu.VMEM((rows, HQ * HD), jnp.bfloat16),
            pltpu.VMEM((NZ * PLANE, HD), jnp.bfloat16),
            pltpu.VMEM((NZ * PLANE, HD), jnp.bfloat16),
            state, state, state,
            pltpu.VMEM((rows, BLOCK), jnp.float32),
            pltpu.VMEM((2, rows, PLANE), jnp.float32),
            pltpu.VMEM((rows, HQ * HD), jnp.bfloat16),
            pltpu.SemaphoreType.DMA((4,)),
            pltpu.SemaphoreType.DMA((n_y,)),
            pltpu.SemaphoreType.DMA((n_y,)),
            pltpu.SemaphoreType.DMA((n_z,)),
            pltpu.SemaphoreType.DMA((n_z,)),
            pltpu.SemaphoreType.DMA((n_x,)),
            pltpu.SemaphoreType.DMA((n_x,)),
        ],
        compiler_params=pltpu.CompilerParams(
            collective_id=0, has_side_effects=True, vmem_limit_bytes=62 * 1024 * 1024
        ),
    )(retrieval, queries, keys, values)


def solution(mesh):
    return jax.shard_map(
        shards,
        mesh=mesh,
        in_specs=(P("ctx", "kv"), P("ctx", "kv"), P("ctx", "kv"), P("kv")),
        out_specs=P(("ctx", "kv"), None),
        check_vma=False,
    )
```

```python
import functools

import jax
import jax.numpy as jnp
from jax import lax
from jax.experimental import pallas as pl
from jax.experimental.pallas import tpu as pltpu
from jax.sharding import PartitionSpec as P

HD = 128
HQ = 8
SINK = 64
WINDOW = 4096
NEG = -1e30
SCALE = HD ** (-0.5) * 1.4426950408889634

NY = 4
NZ = 8
NKV = 8
PARTS = {"k": 2, "v": NY}
BLOCK = 256
PLANE = NY * BLOCK
HALF = BLOCK // 2
GROUPS = 2
WIDE = HQ * HD // GROUPS
MESH = pl.DeviceIdType.MESH


def kernel(
    flags_hbm, q_hbm, k_hbm, v_hbm, out_ref,
    flags, q_ref, kbuf, vbuf, peak, total, numer, own_bias, edge_bias, done,
    local_sem, y_send, y_recv, z_send, z_recv, x_send, x_recv,
):
    ctx = lax.axis_index("ctx")
    kv = lax.axis_index("kv")
    z = ctx // NY
    y = ctx % NY

    def plane(d):
        return (z + d + NZ) % NZ

    def beside(d):
        return (y + d + NY) % NY

    def y_device(d):
        return {"ctx": z * NY + beside(d), "kv": kv}

    def z_device(d):
        return {"ctx": plane(d) * NY + y, "kv": kv}

    def x_device(j):
        return {"ctx": ctx, "kv": (kv + j) % NKV}

    barrier = pltpu.get_barrier_semaphore()

    def greet(peer):
        pl.semaphore_signal(barrier, inc=1, device_id=peer, device_id_type=MESH)

    for d in range(1, NY):
        greet(y_device(d))
    for j in range(1, NKV):
        greet(x_device(j))
    pl.when(z > 0)(functools.partial(greet, z_device(-1)))
    pl.when((z != NZ // 2 - 1))(functools.partial(greet, z_device(1)))
    expected = NY - 1 + NKV - 1 + jnp.where(z < NZ - 1, 1, 0) + jnp.where(z != NZ // 2, 1, 0)

    def rows_of(start, size):
        return pl.ds(pl.multiple_of(start, HALF), size)

    mine = rows_of(ctx * BLOCK, BLOCK)
    local = [
        pltpu.make_async_copy(v_hbm, vbuf.at[mine, :], local_sem.at[0]),
        pltpu.make_async_copy(k_hbm, kbuf.at[mine, :], local_sem.at[1]),
        pltpu.make_async_copy(flags_hbm, flags, local_sem.at[2]),
        pltpu.make_async_copy(q_hbm, q_ref, local_sem.at[3]),
    ]
    for copy in local:
        copy.start()
    pl.semaphore_wait(barrier, expected)

    bufs = {"k": kbuf, "v": vbuf}
    started = {}
    numbers = {}

    def remote(src, dst, peer, sems, key):
        count = len([k for k in numbers if k[0] == key[0]])
        number = numbers.setdefault(key, count)
        return pltpu.make_async_remote_copy(
            src_ref=src,
            dst_ref=dst,
            send_sem=sems[0].at[number],
            recv_sem=sems[1].at[number],
            device_id=peer,
            device_id_type=MESH,
        )

    def y_copy(name, d, way, receive):
        rows = rows_of((plane(d) * NY + (beside(-way) if receive else y)) * BLOCK, BLOCK)
        dst = bufs[name].at[rows, :]
        src = {"k": k_hbm, "v": v_hbm}[name] if d == 0 else dst
        return remote(src, dst, y_device(way), (y_send, y_recv), ("y", name, d, way))

    def z_copy(name, hop, sign, part, receive):
        p = plane(-sign * (hop if receive else hop - 1))
        if name == "k":
            rows = rows_of((p * NY + y) * BLOCK + part * HALF, HALF)
        else:
            rows = rows_of((p * NY + beside(part)) * BLOCK, BLOCK)
        ref = bufs[name].at[rows, :]
        src = ref
        if hop == 1 and not receive:
            if name == "k":
                src = k_hbm.at[pl.ds(part * HALF, HALF), :]
            elif part == 0:
                src = v_hbm
        return remote(src, ref, z_device(sign), (z_send, z_recv), ("z", name, hop, sign, part))

    def last_hop(name, sign, part):
        return NZ // 2 if (part < PARTS[name] // 2) == (sign > 0) else NZ // 2 - 1

    def needed(name, hop, sign, part, receive):
        if sign > 0:
            return z >= hop if receive else (z >= hop - 1) & (z < NZ - 1)
        return plane(hop if receive else hop - 1) < last_hop(name, sign, part)

    def go(maker, *key, when=None):
        def start():
            maker(*key, False).start()

        def end():
            maker(*key, False).wait_send()

        if when is None:
            start()
        else:
            pl.when(when())(start)
        started[(maker, *key)] = (end, when)

    def arrive(maker, *key, when=None):
        def wait():
            maker(*key, True).wait_recv()

        if when is None:
            wait()
        else:
            pl.when(when())(wait)

    def y_wanted(name, back, way, receive):
        if back > 0:
            return z >= back
        later = beside(-way) < y if receive else beside(way) > y
        return later if name == "k" else later | (z < NZ - 1)

    def go_y(name, back):
        for way in (1, -1, 2):
            go(y_copy, name, -back, way, when=functools.partial(y_wanted, name, back, way, False))

    def arrive_y(name, back):
        for way in (1, -1, 2):
            arrive(y_copy, name, -back, way, when=functools.partial(y_wanted, name, back, way, True))

    def send_on(name, hop, sign, part):
        if hop <= last_hop(name, sign, part):
            go(z_copy, name, hop, sign, part, when=functools.partial(needed, name, hop, sign, part, False))

    def pass_on(name, hop):
        for part in range(PARTS[name]):
            for sign in (1, -1):
                if hop <= last_hop(name, sign, part):
                    arrive(z_copy, name, hop, sign, part, when=functools.partial(needed, name, hop, sign, part, True))
                    send_on(name, hop + 1, sign, part)

    go_y("v", 0)
    for sign in (1, -1):
        for part in range(PARTS["k"]):
            send_on("k", 1, sign, part)
        send_on("v", 1, sign, 0)

    peak[...] = jnp.full_like(peak, NEG)
    total[...] = jnp.zeros_like(total)
    numer[...] = jnp.zeros_like(numer)

    def compute(start, size, term, after=None):
        rows = pl.ds(pl.multiple_of(start, BLOCK), size)
        scores, weights, fades = {}, {}, {}

        def score(h):
            scores[h] = lax.dot_general(
                q_ref[:, h * HD:(h + 1) * HD], kbuf[rows, :],
                (((1,), (1,)), ((), ())), preferred_element_type=jnp.float32,
            )

        def weigh(h):
            s = scores.pop(h) + term(h)
            old = peak[h]
            new = jnp.maximum(old, jnp.max(s, axis=1, keepdims=True))
            weights[h] = jnp.exp2(s * SCALE - jnp.tile(new * SCALE, (1, size // HD))).astype(jnp.bfloat16)
            fades[h] = jnp.exp2((old - new) * SCALE)
            peak[h] = new

        def add(h):
            piece = vbuf[rows, :]
            piece = jnp.concatenate([piece, jnp.ones_like(piece)], axis=1)
            sums = jnp.dot(weights.pop(h), piece, preferred_element_type=jnp.float32)
            fade = fades.pop(h)
            total[h] = total[h] * fade + sums[:, HD:]
            numer[h] = numer[h] * fade + sums[:, :HD]

        score(0)
        for h in range(HQ):
            if h + 1 < HQ:
                score(h + 1)
            weigh(h)
            if h > 0:
                add(h - 1)
                if after is not None:
                    after(h - 1)
        add(HQ - 1)
        if after is not None:
            after(HQ - 1)

    edge = z - WINDOW // PLANE

    def shut(h):
        return (1 - flags[h]).astype(jnp.float32) * NEG

    def block_of_own():
        compute(ctx * BLOCK, BLOCK, lambda h: own_bias[...])

    def blocks_before():
        column = lax.broadcasted_iota(jnp.int32, (1, PLANE - BLOCK), 1)
        row = jnp.where(column < y * BLOCK, 0.0, NEG)
        compute(z * PLANE, PLANE - BLOCK, lambda h: row)

    def whole_plane(p):
        column = lax.broadcasted_iota(jnp.int32, (1, PLANE), 1)
        row = jnp.where((p < edge) & (p * PLANE + column >= SINK), 1.0, 0.0)
        compute(p * PLANE, PLANE, lambda h: row * shut(h))

    def edge_plane(after):
        compute(edge * PLANE, PLANE, lambda h: edge_bias[flags[h]], after)

    own_bias[...] = jnp.where(
        lax.broadcasted_iota(jnp.int32, (BLOCK, BLOCK), 1) <= lax.broadcasted_iota(jnp.int32, (BLOCK, BLOCK), 0), 0.0, NEG
    )
    for copy in local:
        copy.wait()
    go_y("k", 0)
    block_of_own()

    def some(i, _):
        rows = pl.ds(pl.multiple_of(i * 32, 32), 32)
        t = y * BLOCK + i * 32 + lax.broadcasted_iota(jnp.int32, (32, PLANE), 0)
        s = lax.broadcasted_iota(jnp.int32, (32, PLANE), 1)
        edge_bias[0, rows, :] = jnp.where((s > t) | (edge * PLANE + s < SINK), 0.0, NEG)
        edge_bias[1, rows, :] = jnp.zeros((32, PLANE), jnp.float32)
        return 0

    lax.fori_loop(0, BLOCK // 32, some, 0)
    pass_on("k", 1)
    go_y("k", 1)
    arrive_y("v", 0)
    for part in range(1, PARTS["v"]):
        for sign in (1, -1):
            send_on("v", 1, sign, part)
    arrive_y("k", 0)
    go_y("k", 7)
    pass_on("k", 2)
    go_y("k", 2)
    go_y("k", 6)
    pl.when(y > 0)(blocks_before)

    def step(i):
        if i == 1:
            pass_on("v", 1)
            arrive_y("k", 1)
        elif i == 2:
            pass_on("k", 3)
            go_y("k", 3)
            go_y("k", 5)
            arrive_y("k", 7)
        elif i == 3:
            pass_on("v", 2)
            pass_on("k", 4)
            go_y("k", 4)
            arrive_y("k", 2)
        elif i == 4:
            arrive_y("k", 6)
        elif i == 5:
            pass_on("v", 3)
            arrive_y("k", 3)
        elif i == 6:
            arrive_y("k", 5)

    def one(i, _):
        for k in range(1, NZ - 1):
            pl.when(i == k)(functools.partial(step, k))
        ring = (i + 1) // 2
        p = (z + jnp.where(i % 2 == 0, ring, -ring) + NZ) % NZ
        pl.when(p < z)(functools.partial(whole_plane, p))
        return 0

    lax.fori_loop(1, NZ - 1, one, 0)

    def x_copy(j, g, receive):
        rows = (kv + j) % NKV * (BLOCK // NKV)
        columns = ((kv - j + NKV) % NKV if receive else kv) * (HQ * HD) + g * WIDE
        return remote(
            done.at[pl.ds(pl.multiple_of(rows, BLOCK // NKV), BLOCK // NKV), pl.ds(g * WIDE, WIDE)],
            out_ref.at[:, pl.ds(pl.multiple_of(columns, WIDE), WIDE)],
            x_device(j), (x_send, x_recv), ("x", j, g),
        )

    def finish(h):
        done[:, h * HD:(h + 1) * HD] = (numer[h] / total[h]).astype(jnp.bfloat16)
        if (h + 1) % (HQ // GROUPS) == 0:
            for j in range(1, NKV):
                go(x_copy, j, h // (HQ // GROUPS))

    pass_on("v", NZ // 2)
    arrive_y("k", 4)

    @pl.when(edge >= 0)
    def _():
        edge_plane(finish)

    @pl.when(edge < 0)
    def _():
        for h in range(HQ):
            finish(h)

    own = pl.ds(pl.multiple_of(kv * (BLOCK // NKV), BLOCK // NKV), BLOCK // NKV)
    out_ref[:, pl.ds(pl.multiple_of(kv * (HQ * HD), HQ * HD), HQ * HD)] = done[own, :]
    def finish_sends(last):
        for (maker, *_), (end, when) in started.items():
            if (maker is x_copy) != last:
                continue
            if when is None:
                end()
            else:
                pl.when(when())(end)

    finish_sends(False)
    for g in range(GROUPS):
        for j in range(1, NKV):
            arrive(x_copy, j, g)
    finish_sends(True)


def shards(queries, keys, values, retrieval):
    rows = queries.shape[0]
    state = pltpu.VMEM((HQ, rows, HD), jnp.float32)
    n_y = (NY - 1) * (1 + NZ)
    n_z = (PARTS["k"] + PARTS["v"]) * 7
    n_x = (NKV - 1) * GROUPS
    return pl.pallas_call(
        kernel,
        out_shape=jax.ShapeDtypeStruct((rows // NKV, NKV * HQ * HD), jnp.bfloat16),
        in_specs=[pl.BlockSpec(memory_space=pltpu.HBM)] * 4,
        out_specs=pl.BlockSpec(memory_space=pltpu.VMEM),
        scratch_shapes=[
            pltpu.SMEM((HQ,), jnp.int32),
            pltpu.VMEM((rows, HQ * HD), jnp.bfloat16),
            pltpu.VMEM((NZ * PLANE, HD), jnp.bfloat16),
            pltpu.VMEM((NZ * PLANE, HD), jnp.bfloat16),
            state, state, state,
            pltpu.VMEM((rows, BLOCK), jnp.float32),
            pltpu.VMEM((2, rows, PLANE), jnp.float32),
            pltpu.VMEM((rows, HQ * HD), jnp.bfloat16),
            pltpu.SemaphoreType.DMA((4,)),
            pltpu.SemaphoreType.DMA((n_y,)),
            pltpu.SemaphoreType.DMA((n_y,)),
            pltpu.SemaphoreType.DMA((n_z,)),
            pltpu.SemaphoreType.DMA((n_z,)),
            pltpu.SemaphoreType.DMA((n_x,)),
            pltpu.SemaphoreType.DMA((n_x,)),
        ],
        compiler_params=pltpu.CompilerParams(
            collective_id=0, has_side_effects=True, vmem_limit_bytes=62 * 1024 * 1024
        ),
    )(retrieval, queries, keys, values)


def solution(mesh):
    return jax.shard_map(
        shards,
        mesh=mesh,
        in_specs=(P("ctx", "kv"), P("ctx", "kv"), P("ctx", "kv"), P("kv")),
        out_specs=P(("ctx", "kv"), None),
        check_vma=False,
    )
```

```python
import functools

import jax
import jax.numpy as jnp
from jax import lax
from jax.experimental import pallas as pl
from jax.experimental.pallas import tpu as pltpu
from jax.sharding import PartitionSpec as P

HD = 128
HQ = 8
SINK = 64
WINDOW = 4096
NEG = -1e30
SCALE = HD ** (-0.5) * 1.4426950408889634

NY = 4
NZ = 8
NKV = 8
PARTS = {"k": 2, "v": NY}
BLOCK = 256
PLANE = NY * BLOCK
HALF = BLOCK // 2
GROUPS = 2
WIDE = HQ * HD // GROUPS
MESH = pl.DeviceIdType.MESH


def kernel(
    flags_hbm, q_hbm, k_hbm, v_hbm, out_ref,
    flags, q_ref, kbuf, vbuf, peak, total, numer, own_bias, edge_bias, done,
    local_sem, y_send, y_recv, z_send, z_recv, x_send, x_recv,
):
    ctx = lax.axis_index("ctx")
    kv = lax.axis_index("kv")
    z = ctx // NY
    y = ctx % NY

    def plane(d):
        return (z + d + NZ) % NZ

    def beside(d):
        return (y + d + NY) % NY

    def y_device(d):
        return {"ctx": z * NY + beside(d), "kv": kv}

    def z_device(d):
        return {"ctx": plane(d) * NY + y, "kv": kv}

    def x_device(j):
        return {"ctx": ctx, "kv": (kv + j) % NKV}

    barrier = pltpu.get_barrier_semaphore()

    def greet(peer):
        pl.semaphore_signal(barrier, inc=1, device_id=peer, device_id_type=MESH)

    for d in range(1, NY):
        greet(y_device(d))
    for j in range(1, NKV):
        greet(x_device(j))
    pl.when(z > 0)(functools.partial(greet, z_device(-1)))
    pl.when((z != NZ // 2 - 1))(functools.partial(greet, z_device(1)))
    expected = NY - 1 + NKV - 1 + jnp.where(z < NZ - 1, 1, 0) + jnp.where(z != NZ // 2, 1, 0)

    def rows_of(start, size):
        return pl.ds(pl.multiple_of(start, HALF), size)

    mine = rows_of(ctx * BLOCK, BLOCK)
    local = [
        pltpu.make_async_copy(v_hbm, vbuf.at[mine, :], local_sem.at[0]),
        pltpu.make_async_copy(k_hbm, kbuf.at[mine, :], local_sem.at[1]),
        pltpu.make_async_copy(flags_hbm, flags, local_sem.at[2]),
        pltpu.make_async_copy(q_hbm, q_ref, local_sem.at[3]),
    ]
    for copy in local:
        copy.start()
    pl.semaphore_wait(barrier, expected)

    bufs = {"k": kbuf, "v": vbuf}
    started = {}
    numbers = {}

    def remote(src, dst, peer, sems, key):
        count = len([k for k in numbers if k[0] == key[0]])
        number = numbers.setdefault(key, count)
        return pltpu.make_async_remote_copy(
            src_ref=src,
            dst_ref=dst,
            send_sem=sems[0].at[number],
            recv_sem=sems[1].at[number],
            device_id=peer,
            device_id_type=MESH,
        )

    def y_copy(name, d, way, receive):
        rows = rows_of((plane(d) * NY + (beside(-way) if receive else y)) * BLOCK, BLOCK)
        dst = bufs[name].at[rows, :]
        src = {"k": k_hbm, "v": v_hbm}[name] if d == 0 else dst
        return remote(src, dst, y_device(way), (y_send, y_recv), ("y", name, d, way))

    def z_copy(name, hop, sign, part, receive):
        p = plane(-sign * (hop if receive else hop - 1))
        if name == "k":
            rows = rows_of((p * NY + y) * BLOCK + part * HALF, HALF)
        else:
            rows = rows_of((p * NY + beside(part)) * BLOCK, BLOCK)
        ref = bufs[name].at[rows, :]
        src = ref
        if hop == 1 and not receive:
            if name == "k":
                src = k_hbm.at[pl.ds(part * HALF, HALF), :]
            elif part == 0:
                src = v_hbm
        return remote(src, ref, z_device(sign), (z_send, z_recv), ("z", name, hop, sign, part))

    def last_hop(name, sign, part):
        return NZ // 2 if (part < PARTS[name] // 2) == (sign > 0) else NZ // 2 - 1

    def needed(name, hop, sign, part, receive):
        if sign > 0:
            return z >= hop if receive else (z >= hop - 1) & (z < NZ - 1)
        return plane(hop if receive else hop - 1) < last_hop(name, sign, part)

    def go(maker, *key, when=None):
        def start():
            maker(*key, False).start()

        def end():
            maker(*key, False).wait_send()

        if when is None:
            start()
        else:
            pl.when(when())(start)
        started[(maker, *key)] = (end, when)

    def arrive(maker, *key, when=None):
        def wait():
            maker(*key, True).wait_recv()

        if when is None:
            wait()
        else:
            pl.when(when())(wait)

    def y_wanted(name, back, way, receive):
        if back > 0:
            return z >= back
        later = beside(-way) < y if receive else beside(way) > y
        return later if name == "k" else later | (z < NZ - 1)

    def go_y(name, back):
        for way in (1, -1, 2):
            go(y_copy, name, -back, way, when=functools.partial(y_wanted, name, back, way, False))

    def arrive_y(name, back):
        for way in (1, -1, 2):
            arrive(y_copy, name, -back, way, when=functools.partial(y_wanted, name, back, way, True))

    def send_on(name, hop, sign, part):
        if hop <= last_hop(name, sign, part):
            go(z_copy, name, hop, sign, part, when=functools.partial(needed, name, hop, sign, part, False))

    def pass_on(name, hop):
        for part in range(PARTS[name]):
            for sign in (1, -1):
                if hop <= last_hop(name, sign, part):
                    arrive(z_copy, name, hop, sign, part, when=functools.partial(needed, name, hop, sign, part, True))
                    send_on(name, hop + 1, sign, part)

    go_y("v", 0)
    for sign in (1, -1):
        for part in range(PARTS["k"]):
            send_on("k", 1, sign, part)
        send_on("v", 1, sign, 0)

    peak[...] = jnp.full_like(peak, NEG)
    total[...] = jnp.zeros_like(total)
    numer[...] = jnp.zeros_like(numer)

    def compute(start, size, term, after=None):
        rows = pl.ds(pl.multiple_of(start, BLOCK), size)
        scores, weights, fades = {}, {}, {}

        def score(h):
            scores[h] = lax.dot_general(
                q_ref[:, h * HD:(h + 1) * HD], kbuf[rows, :],
                (((1,), (1,)), ((), ())), preferred_element_type=jnp.float32,
            )

        def weigh(h):
            s = scores.pop(h) + term(h)
            old = peak[h]
            new = jnp.maximum(old, jnp.max(s, axis=1, keepdims=True))
            weights[h] = jnp.exp2(s * SCALE - jnp.tile(new * SCALE, (1, size // HD))).astype(jnp.bfloat16)
            fades[h] = jnp.exp2((old - new) * SCALE)
            peak[h] = new

        def add(h):
            piece = vbuf[rows, :]
            piece = jnp.concatenate([piece, jnp.ones_like(piece)], axis=1)
            sums = jnp.dot(weights.pop(h), piece, preferred_element_type=jnp.float32)
            fade = fades.pop(h)
            total[h] = total[h] * fade + sums[:, HD:]
            numer[h] = numer[h] * fade + sums[:, :HD]

        score(0)
        for h in range(HQ):
            if h + 1 < HQ:
                score(h + 1)
            weigh(h)
            if h > 0:
                add(h - 1)
                if after is not None:
                    after(h - 1)
        add(HQ - 1)
        if after is not None:
            after(HQ - 1)

    edge = z - WINDOW // PLANE

    def shut(h):
        return (1 - flags[h]).astype(jnp.float32) * NEG

    def block_of_own():
        compute(ctx * BLOCK, BLOCK, lambda h: own_bias[...])

    def blocks_before():
        column = lax.broadcasted_iota(jnp.int32, (1, PLANE - BLOCK), 1)
        row = jnp.where(column < y * BLOCK, 0.0, NEG)
        compute(z * PLANE, PLANE - BLOCK, lambda h: row)

    def whole_plane(p):
        column = lax.broadcasted_iota(jnp.int32, (1, PLANE), 1)
        row = jnp.where((p < edge) & (p * PLANE + column >= SINK), 1.0, 0.0)
        compute(p * PLANE, PLANE, lambda h: row * shut(h))

    def edge_plane(after):
        compute(edge * PLANE, PLANE, lambda h: edge_bias[flags[h]], after)

    own_bias[...] = jnp.where(
        lax.broadcasted_iota(jnp.int32, (BLOCK, BLOCK), 1) <= lax.broadcasted_iota(jnp.int32, (BLOCK, BLOCK), 0), 0.0, NEG
    )
    for copy in local:
        copy.wait()
    go_y("k", 0)
    block_of_own()

    def some(i, _):
        rows = pl.ds(pl.multiple_of(i * 32, 32), 32)
        t = y * BLOCK + i * 32 + lax.broadcasted_iota(jnp.int32, (32, PLANE), 0)
        s = lax.broadcasted_iota(jnp.int32, (32, PLANE), 1)
        edge_bias[0, rows, :] = jnp.where((s > t) | (edge * PLANE + s < SINK), 0.0, NEG)
        edge_bias[1, rows, :] = jnp.zeros((32, PLANE), jnp.float32)
        return 0

    lax.fori_loop(0, BLOCK // 32, some, 0)
    pass_on("k", 1)
    go_y("k", 1)
    arrive_y("v", 0)
    for part in range(1, PARTS["v"]):
        for sign in (1, -1):
            send_on("v", 1, sign, part)
    arrive_y("k", 0)
    go_y("k", 7)
    pass_on("k", 2)
    go_y("k", 2)
    go_y("k", 6)
    pl.when(y > 0)(blocks_before)

    def step(i):
        if i == 1:
            pass_on("v", 1)
            arrive_y("k", 1)
        elif i == 2:
            pass_on("k", 3)
            go_y("k", 3)
            go_y("k", 5)
            arrive_y("k", 7)
        elif i == 3:
            pass_on("v", 2)
            pass_on("k", 4)
            go_y("k", 4)
            arrive_y("k", 2)
        elif i == 4:
            arrive_y("k", 6)
        elif i == 5:
            pass_on("v", 3)
            arrive_y("k", 3)
        elif i == 6:
            arrive_y("k", 5)

    def one(i, _):
        for k in range(1, NZ - 1):
            pl.when(i == k)(functools.partial(step, k))
        ring = (i + 1) // 2
        p = (z + jnp.where(i % 2 == 0, ring, -ring) + NZ) % NZ
        pl.when(p < z)(functools.partial(whole_plane, p))
        return 0

    lax.fori_loop(1, NZ - 1, one, 0)

    def x_copy(j, g, receive):
        rows = (kv + j) % NKV * (BLOCK // NKV)
        columns = ((kv - j + NKV) % NKV if receive else kv) * (HQ * HD) + g * WIDE
        return remote(
            done.at[pl.ds(pl.multiple_of(rows, BLOCK // NKV), BLOCK // NKV), pl.ds(g * WIDE, WIDE)],
            out_ref.at[:, pl.ds(pl.multiple_of(columns, WIDE), WIDE)],
            x_device(j), (x_send, x_recv), ("x", j, g),
        )

    def finish(h):
        done[:, h * HD:(h + 1) * HD] = (numer[h] / total[h]).astype(jnp.bfloat16)
        if (h + 1) % (HQ // GROUPS) == 0:
            for j in range(1, NKV):
                go(x_copy, j, h // (HQ // GROUPS))

    pass_on("v", NZ // 2)
    arrive_y("k", 4)

    @pl.when(edge >= 0)
    def _():
        edge_plane(finish)

    @pl.when(edge < 0)
    def _():
        for h in range(HQ):
            finish(h)

    own = pl.ds(pl.multiple_of(kv * (BLOCK // NKV), BLOCK // NKV), BLOCK // NKV)
    keep = pltpu.make_async_copy(
        done.at[own, :], out_ref.at[:, pl.ds(pl.multiple_of(kv * (HQ * HD), HQ * HD), HQ * HD)], local_sem.at[4]
    )
    keep.start()
    def finish_sends(last):
        for (maker, *_), (end, when) in started.items():
            if (maker is x_copy) != last:
                continue
            if when is None:
                end()
            else:
                pl.when(when())(end)

    finish_sends(False)
    for g in range(GROUPS):
        for j in range(1, NKV):
            arrive(x_copy, j, g)
    keep.wait()
    finish_sends(True)


def shards(queries, keys, values, retrieval):
    rows = queries.shape[0]
    state = pltpu.VMEM((HQ, rows, HD), jnp.float32)
    n_y = (NY - 1) * (1 + NZ)
    n_z = (PARTS["k"] + PARTS["v"]) * 7
    n_x = (NKV - 1) * GROUPS
    return pl.pallas_call(
        kernel,
        out_shape=jax.ShapeDtypeStruct((rows // NKV, NKV * HQ * HD), jnp.bfloat16),
        in_specs=[pl.BlockSpec(memory_space=pltpu.HBM)] * 4,
        out_specs=pl.BlockSpec(memory_space=pltpu.HBM),
        scratch_shapes=[
            pltpu.SMEM((HQ,), jnp.int32),
            pltpu.VMEM((rows, HQ * HD), jnp.bfloat16),
            pltpu.VMEM((NZ * PLANE, HD), jnp.bfloat16),
            pltpu.VMEM((NZ * PLANE, HD), jnp.bfloat16),
            state, state, state,
            pltpu.VMEM((rows, BLOCK), jnp.float32),
            pltpu.VMEM((2, rows, PLANE), jnp.float32),
            pltpu.VMEM((rows, HQ * HD), jnp.bfloat16),
            pltpu.SemaphoreType.DMA((5,)),
            pltpu.SemaphoreType.DMA((n_y,)),
            pltpu.SemaphoreType.DMA((n_y,)),
            pltpu.SemaphoreType.DMA((n_z,)),
            pltpu.SemaphoreType.DMA((n_z,)),
            pltpu.SemaphoreType.DMA((n_x,)),
            pltpu.SemaphoreType.DMA((n_x,)),
        ],
        compiler_params=pltpu.CompilerParams(
            collective_id=0, has_side_effects=True, vmem_limit_bytes=62 * 1024 * 1024
        ),
    )(retrieval, queries, keys, values)


def solution(mesh):
    return jax.shard_map(
        shards,
        mesh=mesh,
        in_specs=(P("ctx", "kv"), P("ctx", "kv"), P("ctx", "kv"), P("kv")),
        out_specs=P(("ctx", "kv"), None),
        check_vma=False,
    )
```

```python
import functools

import jax
import jax.numpy as jnp
from jax import lax
from jax.experimental import pallas as pl
from jax.experimental.pallas import tpu as pltpu
from jax.sharding import PartitionSpec as P

HD = 128
HQ = 8
SINK = 64
WINDOW = 4096
NEG = -1e30
SCALE = HD ** (-0.5) * 1.4426950408889634

NY = 4
NZ = 8
NKV = 8
PARTS = {"k": 2, "v": NY}
BLOCK = 256
PLANE = NY * BLOCK
HALF = BLOCK // 2
GROUPS = 2
WIDE = HQ * HD // GROUPS
MESH = pl.DeviceIdType.MESH


def kernel(
    flags_hbm, q_hbm, k_hbm, v_hbm, out_ref,
    flags, q_ref, kbuf, vbuf, peak, total, numer, own_bias, edge_bias, done,
    local_sem, y_send, y_recv, z_send, z_recv, x_send, x_recv,
):
    ctx = lax.axis_index("ctx")
    kv = lax.axis_index("kv")
    z = ctx // NY
    y = ctx % NY

    def plane(d):
        return (z + d + NZ) % NZ

    def beside(d):
        return (y + d + NY) % NY

    def y_device(d):
        return {"ctx": z * NY + beside(d), "kv": kv}

    def z_device(d):
        return {"ctx": plane(d) * NY + y, "kv": kv}

    def x_device(j):
        return {"ctx": ctx, "kv": (kv + j) % NKV}

    barrier = pltpu.get_barrier_semaphore()

    def greet(peer):
        pl.semaphore_signal(barrier, inc=1, device_id=peer, device_id_type=MESH)

    for d in range(1, NY):
        greet(y_device(d))
    for j in range(1, NKV):
        greet(x_device(j))
    pl.when(z > 0)(functools.partial(greet, z_device(-1)))
    pl.when((z != NZ // 2 - 1))(functools.partial(greet, z_device(1)))
    expected = NY - 1 + NKV - 1 + jnp.where(z < NZ - 1, 1, 0) + jnp.where(z != NZ // 2, 1, 0)

    def rows_of(start, size):
        return pl.ds(pl.multiple_of(start, HALF), size)

    mine = rows_of(ctx * BLOCK, BLOCK)
    local = [
        pltpu.make_async_copy(v_hbm, vbuf.at[mine, :], local_sem.at[0]),
        pltpu.make_async_copy(k_hbm, kbuf.at[mine, :], local_sem.at[1]),
        pltpu.make_async_copy(flags_hbm, flags, local_sem.at[2]),
        pltpu.make_async_copy(q_hbm, q_ref, local_sem.at[3]),
    ]
    for copy in local:
        copy.start()
    pl.semaphore_wait(barrier, expected)

    bufs = {"k": kbuf, "v": vbuf}
    started = {}
    numbers = {}

    def remote(src, dst, peer, sems, key):
        count = len([k for k in numbers if k[0] == key[0]])
        number = numbers.setdefault(key, count)
        return pltpu.make_async_remote_copy(
            src_ref=src,
            dst_ref=dst,
            send_sem=sems[0].at[number],
            recv_sem=sems[1].at[number],
            device_id=peer,
            device_id_type=MESH,
        )

    def y_copy(name, d, way, receive):
        rows = rows_of((plane(d) * NY + (beside(-way) if receive else y)) * BLOCK, BLOCK)
        dst = bufs[name].at[rows, :]
        src = {"k": k_hbm, "v": v_hbm}[name] if d == 0 else dst
        return remote(src, dst, y_device(way), (y_send, y_recv), ("y", name, d, way))

    def z_copy(name, hop, sign, part, receive):
        p = plane(-sign * (hop if receive else hop - 1))
        if name == "k":
            rows = rows_of((p * NY + y) * BLOCK + part * HALF, HALF)
        else:
            rows = rows_of((p * NY + beside(part)) * BLOCK, BLOCK)
        ref = bufs[name].at[rows, :]
        src = ref
        if hop == 1 and not receive:
            if name == "k":
                src = k_hbm.at[pl.ds(part * HALF, HALF), :]
            elif part == 0:
                src = v_hbm
        return remote(src, ref, z_device(sign), (z_send, z_recv), ("z", name, hop, sign, part))

    def last_hop(name, sign, part):
        return NZ // 2 if (part < PARTS[name] // 2) == (sign > 0) else NZ // 2 - 1

    def needed(name, hop, sign, part, receive):
        if sign > 0:
            return z >= hop if receive else (z >= hop - 1) & (z < NZ - 1)
        return plane(hop if receive else hop - 1) < last_hop(name, sign, part)

    def go(maker, *key, when=None):
        def start():
            maker(*key, False).start()

        def end():
            maker(*key, False).wait_send()

        if when is None:
            start()
        else:
            pl.when(when())(start)
        started[(maker, *key)] = (end, when)

    def arrive(maker, *key, when=None):
        def wait():
            maker(*key, True).wait_recv()

        if when is None:
            wait()
        else:
            pl.when(when())(wait)

    def y_wanted(name, back, way, receive):
        if back > 0:
            return z >= back
        later = beside(-way) < y if receive else beside(way) > y
        return later if name == "k" else later | (z < NZ - 1)

    def go_y(name, back):
        for way in (1, -1, 2):
            go(y_copy, name, -back, way, when=functools.partial(y_wanted, name, back, way, False))

    def arrive_y(name, back):
        for way in (1, -1, 2):
            arrive(y_copy, name, -back, way, when=functools.partial(y_wanted, name, back, way, True))

    def send_on(name, hop, sign, part):
        if hop <= last_hop(name, sign, part):
            go(z_copy, name, hop, sign, part, when=functools.partial(needed, name, hop, sign, part, False))

    def pass_on(name, hop):
        for part in range(PARTS[name]):
            for sign in (1, -1):
                if hop <= last_hop(name, sign, part):
                    arrive(z_copy, name, hop, sign, part, when=functools.partial(needed, name, hop, sign, part, True))
                    send_on(name, hop + 1, sign, part)

    go_y("v", 0)
    for sign in (1, -1):
        for part in range(PARTS["k"]):
            send_on("k", 1, sign, part)
        send_on("v", 1, sign, 0)

    peak[...] = jnp.full_like(peak, NEG)
    total[...] = jnp.zeros_like(total)
    numer[...] = jnp.zeros_like(numer)

    def compute(start, size, term, after=None, bar=None):
        rows = pl.ds(pl.multiple_of(start, BLOCK), size)
        scores, weights, fades = {}, {}, {}

        def score(h):
            scores[h] = lax.dot_general(
                q_ref[:, h * HD:(h + 1) * HD], kbuf[rows, :],
                (((1,), (1,)), ((), ())), preferred_element_type=jnp.float32,
            )

        def weigh(h):
            s = scores.pop(h)
            old = peak[h]
            if bar is None:
                s = s + term(h)
                new = jnp.maximum(old, jnp.max(s, axis=1, keepdims=True))
                low = new * SCALE
            else:
                new = jnp.maximum(old, jnp.max(s, axis=1, keepdims=True) + bar(h))
                low = new * SCALE - bar(h)
            weights[h] = jnp.exp2(s * SCALE - jnp.tile(low, (1, size // HD))).astype(jnp.bfloat16)
            fades[h] = jnp.exp2((old - new) * SCALE)
            peak[h] = new

        def add(h):
            piece = vbuf[rows, :]
            piece = jnp.concatenate([piece, jnp.ones_like(piece)], axis=1)
            sums = jnp.dot(weights.pop(h), piece, preferred_element_type=jnp.float32)
            fade = fades.pop(h)
            total[h] = total[h] * fade + sums[:, HD:]
            numer[h] = numer[h] * fade + sums[:, :HD]

        score(0)
        for h in range(HQ):
            if h + 1 < HQ:
                score(h + 1)
            weigh(h)
            if h > 0:
                add(h - 1)
                if after is not None:
                    after(h - 1)
        add(HQ - 1)
        if after is not None:
            after(HQ - 1)

    edge = z - WINDOW // PLANE

    def shut(h):
        return (1 - flags[h]).astype(jnp.float32) * NEG

    def block_of_own():
        compute(ctx * BLOCK, BLOCK, lambda h: own_bias[...])

    def blocks_before():
        column = lax.broadcasted_iota(jnp.int32, (1, PLANE - BLOCK), 1)
        row = jnp.where(column < y * BLOCK, 0.0, NEG)
        compute(z * PLANE, PLANE - BLOCK, lambda h: row)

    def whole_plane(p):
        column = lax.broadcasted_iota(jnp.int32, (1, PLANE), 1)
        row = jnp.where((p < edge) & (p * PLANE + column >= SINK), 1.0, 0.0)
        sink = (p == 0) & (edge > 0)

        @pl.when(sink)
        def _():
            compute(p * PLANE, PLANE, lambda h: row * shut(h))

        @pl.when(jnp.logical_not(sink))
        def _():
            compute(p * PLANE, PLANE, None, bar=lambda h: jnp.where(p < edge, shut(h), 0.0))

    def edge_plane(after):
        compute(edge * PLANE, PLANE, lambda h: edge_bias[flags[h]], after)

    own_bias[...] = jnp.where(
        lax.broadcasted_iota(jnp.int32, (BLOCK, BLOCK), 1) <= lax.broadcasted_iota(jnp.int32, (BLOCK, BLOCK), 0), 0.0, NEG
    )
    for copy in local:
        copy.wait()
    go_y("k", 0)
    block_of_own()

    def some(i, _):
        rows = pl.ds(pl.multiple_of(i * 32, 32), 32)
        t = y * BLOCK + i * 32 + lax.broadcasted_iota(jnp.int32, (32, PLANE), 0)
        s = lax.broadcasted_iota(jnp.int32, (32, PLANE), 1)
        edge_bias[0, rows, :] = jnp.where((s > t) | (edge * PLANE + s < SINK), 0.0, NEG)
        edge_bias[1, rows, :] = jnp.zeros((32, PLANE), jnp.float32)
        return 0

    lax.fori_loop(0, BLOCK // 32, some, 0)
    pass_on("k", 1)
    go_y("k", 1)
    arrive_y("v", 0)
    for part in range(1, PARTS["v"]):
        for sign in (1, -1):
            send_on("v", 1, sign, part)
    arrive_y("k", 0)
    go_y("k", 7)
    pass_on("k", 2)
    go_y("k", 2)
    go_y("k", 6)
    pl.when(y > 0)(blocks_before)

    def step(i):
        if i == 1:
            pass_on("v", 1)
            arrive_y("k", 1)
        elif i == 2:
            pass_on("k", 3)
            go_y("k", 3)
            go_y("k", 5)
            arrive_y("k", 7)
        elif i == 3:
            pass_on("v", 2)
            pass_on("k", 4)
            go_y("k", 4)
            arrive_y("k", 2)
        elif i == 4:
            arrive_y("k", 6)
        elif i == 5:
            pass_on("v", 3)
            arrive_y("k", 3)
        elif i == 6:
            arrive_y("k", 5)

    def one(i, _):
        for k in range(1, NZ - 1):
            pl.when(i == k)(functools.partial(step, k))
        ring = (i + 1) // 2
        p = (z + jnp.where(i % 2 == 0, ring, -ring) + NZ) % NZ
        pl.when(p < z)(functools.partial(whole_plane, p))
        return 0

    lax.fori_loop(1, NZ - 1, one, 0)

    def x_copy(j, g, receive):
        rows = (kv + j) % NKV * (BLOCK // NKV)
        columns = ((kv - j + NKV) % NKV if receive else kv) * (HQ * HD) + g * WIDE
        return remote(
            done.at[pl.ds(pl.multiple_of(rows, BLOCK // NKV), BLOCK // NKV), pl.ds(g * WIDE, WIDE)],
            out_ref.at[:, pl.ds(pl.multiple_of(columns, WIDE), WIDE)],
            x_device(j), (x_send, x_recv), ("x", j, g),
        )

    def finish(h):
        done[:, h * HD:(h + 1) * HD] = (numer[h] / total[h]).astype(jnp.bfloat16)
        if (h + 1) % (HQ // GROUPS) == 0:
            for j in (4, 3, 5, 2, 6, 1, 7):
                go(x_copy, j, h // (HQ // GROUPS))

    pass_on("v", NZ // 2)
    arrive_y("k", 4)

    @pl.when(edge >= 0)
    def _():
        edge_plane(finish)

    @pl.when(edge < 0)
    def _():
        for h in range(HQ):
            finish(h)

    own = pl.ds(pl.multiple_of(kv * (BLOCK // NKV), BLOCK // NKV), BLOCK // NKV)
    keep = pltpu.make_async_copy(
        done.at[own, :], out_ref.at[:, pl.ds(pl.multiple_of(kv * (HQ * HD), HQ * HD), HQ * HD)], local_sem.at[4]
    )
    keep.start()
    def finish_sends(last):
        for (maker, *_), (end, when) in started.items():
            if (maker is x_copy) != last:
                continue
            if when is None:
                end()
            else:
                pl.when(when())(end)

    finish_sends(False)
    for g in range(GROUPS):
        for j in range(1, NKV):
            arrive(x_copy, j, g)
    keep.wait()
    finish_sends(True)


def shards(queries, keys, values, retrieval):
    rows = queries.shape[0]
    state = pltpu.VMEM((HQ, rows, HD), jnp.float32)
    n_y = (NY - 1) * (1 + NZ)
    n_z = (PARTS["k"] + PARTS["v"]) * 7
    n_x = (NKV - 1) * GROUPS
    return pl.pallas_call(
        kernel,
        out_shape=jax.ShapeDtypeStruct((rows // NKV, NKV * HQ * HD), jnp.bfloat16),
        in_specs=[pl.BlockSpec(memory_space=pltpu.HBM)] * 4,
        out_specs=pl.BlockSpec(memory_space=pltpu.HBM),
        scratch_shapes=[
            pltpu.SMEM((HQ,), jnp.int32),
            pltpu.VMEM((rows, HQ * HD), jnp.bfloat16),
            pltpu.VMEM((NZ * PLANE, HD), jnp.bfloat16),
            pltpu.VMEM((NZ * PLANE, HD), jnp.bfloat16),
            state, state, state,
            pltpu.VMEM((rows, BLOCK), jnp.float32),
            pltpu.VMEM((2, rows, PLANE), jnp.float32),
            pltpu.VMEM((rows, HQ * HD), jnp.bfloat16),
            pltpu.SemaphoreType.DMA((5,)),
            pltpu.SemaphoreType.DMA((n_y,)),
            pltpu.SemaphoreType.DMA((n_y,)),
            pltpu.SemaphoreType.DMA((n_z,)),
            pltpu.SemaphoreType.DMA((n_z,)),
            pltpu.SemaphoreType.DMA((n_x,)),
            pltpu.SemaphoreType.DMA((n_x,)),
        ],
        compiler_params=pltpu.CompilerParams(
            collective_id=0, has_side_effects=True, vmem_limit_bytes=62 * 1024 * 1024
        ),
    )(retrieval, queries, keys, values)


def solution(mesh):
    return jax.shard_map(
        shards,
        mesh=mesh,
        in_specs=(P("ctx", "kv"), P("ctx", "kv"), P("ctx", "kv"), P("kv")),
        out_specs=P(("ctx", "kv"), None),
        check_vma=False,
    )
```
